768 devices in a mesh: row: 64 (over x, y, core), col: 12 (over z).
Axes of the slice: x: 4, y: 8, z: 12, core: 2. Of those that a mesh axis runs over, the one named last changes fastest.
Arguments:
- momentum: float32 [16384, 13824], P('row', 'col'), may hold values from -0.6 to 0.6
- gradient: bfloat16 [16384, 13824], P('row', 'col'), may hold values from -36 to 36
- right_factor: float32 [13824, 256], P('col'), may hold values from -0.0546875 to 0.0546875
Outputs:
- new_momentum: float32 [16384, 13824], P('row', 'col')
- new_right: float32 [13824, 256], P('col')
- update: bfloat16 [16384, 13824], P('row', 'col')
The draws below stay inside these ranges and needn't reach their ends.
All inputs are finite; a program needn't handle non-finite values.
Results may differ from the reference program's by a relative error of at most 0.001.
Values sent between devices are 32-bit elements; how exact they have to be, the bound alone decides.
No kernel may reach another device: no remote copies, remote signals or barrier semaphores. Data moves between devices by JAX's collectives and lax.ppermute only.
A program may use at most 32 MiB of HBM per device.

```python
import math
import jax
import jax.numpy as jnp
from jax import lax

ROWS = 16384
COLS = 13824
RANK = 256


def draw_gradient(key, part):
    key = jax.random.fold_in(key, 7)
    keys = jax.random.split(key, 3)
    row_ramp = jnp.exp(jnp.arange(ROWS, dtype=jnp.float32)[:, None] * (math.log(3.0) / (ROWS - 1)))
    col_ramp = jnp.exp(jnp.arange(COLS, dtype=jnp.float32)[None, :] * (math.log(3.0) / (COLS - 1)))
    row_scale = jnp.exp(jax.random.uniform(keys[0], (ROWS, 1), jnp.float32) * math.log(10.0)) * row_ramp
    col_scale = jnp.exp(jax.random.uniform(keys[1], (1, COLS), jnp.float32) * math.log(10.0)) * col_ramp
    noise_part = jnp.clip(jax.random.normal(keys[2], (ROWS, COLS), jnp.float32), -4.0, 4.0)
    return (noise_part * row_scale * col_scale * 0.01).astype(jnp.bfloat16)


def block_scale(rng, shape, pieces, smallest, largest):
    def one(position, parts):
        draws = jax.random.uniform(jax.random.fold_in(jax.random.fold_in(rng, 6), position), (parts,), jnp.float32, smallest / len(pieces), largest / len(pieces))
        return jnp.repeat(jnp.exp(draws), shape[position] // parts).reshape((-1,) + (1,) * (len(shape) - position - 1))

    level = one(*pieces[0])
    for cut in pieces[1:]:
        level = level * one(*cut)
    return level


def bell_draw(key, extent, scale, most, cuts=(), kind=jnp.bfloat16):
    result = jax.random.normal(key, extent, jnp.float32) * scale
    if len(cuts) > 0:
        result = block_scale(key, extent, cuts, -0.22, 0.18) * result
    return jnp.clip(result, min=-most, max=most).astype(kind)


def setup_inputs(seed: int = 0) -> dict:
    key_list = jax.random.split(jax.random.key(seed), 4)
    momentum = bell_draw(key_list[0], (ROWS, COLS), 0.1, 0.6, ((0, 64), (1, 12)), jnp.float32)
    gradient = draw_gradient(jax.random.fold_in(key_list[3], 71), 0)
    right_factor = bell_draw(key_list[2], (COLS, RANK), COLS ** -0.5, 0.0546875, ((0, 12),), jnp.float32)
    return dict(momentum=momentum, gradient=gradient, right_factor=right_factor)


decay_rate = 0.95
epsilon = 1e-06

def reference(momentum, gradient, right_factor):
    highest = lax.Precision.HIGHEST
    blended = momentum + gradient.astype(jnp.float32)
    left_raw = jnp.dot(blended.astype(jnp.float32), right_factor.astype(jnp.float32), precision=highest, preferred_element_type=jnp.float32)
    gram_matrix = jnp.dot(left_raw.T.astype(jnp.float32), left_raw.astype(jnp.float32), precision=highest, preferred_element_type=jnp.float32)
    lower_factor = jnp.linalg.cholesky(gram_matrix)
    orthonormal = jax.scipy.linalg.solve_triangular(lower_factor, left_raw.T, lower=True).T
    right_full = jnp.dot(blended.T.astype(jnp.float32), orthonormal.astype(jnp.float32), precision=highest, preferred_element_type=jnp.float32)
    new_momentum = blended - (1.0 - decay_rate) * jnp.dot(orthonormal.astype(jnp.float32), right_full.T.astype(jnp.float32), precision=highest, preferred_element_type=jnp.float32)
    squares = lax.optimization_barrier(jnp.sum(right_full * right_full, axis=0))
    new_right = right_full / jnp.sqrt(squares + epsilon)
    factor = math.sqrt(ROWS * COLS / RANK)
    update = (factor * jnp.dot(orthonormal.astype(jnp.float32), new_right.T.astype(jnp.float32), precision=highest, preferred_element_type=jnp.float32)).astype(jnp.bfloat16)
    return (new_momentum, new_right, update)
```

```python
import math

import jax
import jax.numpy as jnp
from jax import lax
from jax.experimental import pallas as pl
from jax.experimental.pallas import tpu as pltpu
from jax.sharding import Mesh
from jax.sharding import PartitionSpec as P

ROWS = 16384
COLS = 13824
RANK = 256
BLOCK = 32

decay_rate = 0.95
epsilon = 1e-06

ROW = ("x", "y", "core")
SWAP = ((0, 1), (1, 0))
HIGHEST = lax.Precision.HIGHEST


def dot(a, b, contract):
    return lax.dot_general(
        a, b, ((contract[0], contract[1]), ((), ())), precision=HIGHEST, preferred_element_type=jnp.float32
    )


def exchange(parts, axes):
    return lax.all_to_all(parts, axes, 0, 0, tiled=True)


def scatter_sum(parts, axes):
    return jnp.sum(exchange(parts, axes), axis=0)


def gather(part, axes, count):
    return exchange(jnp.broadcast_to(part, (count,) + part.shape), axes)


def wide(a):
    return jnp.concatenate([a, a], axis=1)


def invert_panel(panel, low):
    pieces = len(panel)
    row8 = lax.broadcasted_iota(jnp.int32, (8, 128), 0)
    lane = lax.broadcasted_iota(jnp.int32, (8, 128), 1)
    unit = [(row8 + 8 * r == lane).astype(jnp.float32) for r in range(pieces)]
    scales = []
    for g in range(pieces):
        columns = []
        for i in range(8):
            at = low + 8 * g + i
            columns.append([
                jnp.broadcast_to(panel[r][:, at : at + 1], (8, 128)) if r >= g else None for r in range(pieces)
            ])
        pivots = jnp.zeros((8, 128), jnp.float32)
        factors = []
        for i in range(8):
            pivot = columns[i][g][i : i + 1, :]
            pivots = jnp.where(row8 == i, pivot, pivots)
            inverse = 1.0 / pivot
            factor = [columns[i][r] * inverse if r >= g else None for r in range(pieces)]
            factor[g] = jnp.where(row8 > i, factor[g], 0.0)
            factors.append(factor)
            for l in range(i + 1, 8):
                head = columns[l][g][i : i + 1, :]
                for r in range(g, pieces):
                    columns[l][r] = columns[l][r] - factor[r] * head
        for i in range(8):
            panel_row = panel[g][i : i + 1, :]
            unit_row = unit[g][i : i + 1, :]
            for r in range(g, pieces):
                panel[r] = panel[r] - wide(factors[i][r]) * panel_row
                unit[r] = unit[r] - factors[i][r] * unit_row
        scales.append(lax.rsqrt(pivots))
    panel = [panel[r] * wide(scales[r]) for r in range(pieces)]
    unit = [unit[r] * scales[r] for r in range(pieces)]
    return panel, unit


def split3(a):
    high = a.astype(jnp.bfloat16)
    rest = a - high.astype(jnp.float32)
    middle = rest.astype(jnp.bfloat16)
    return high, middle, (rest - middle.astype(jnp.float32)).astype(jnp.bfloat16)


def invert_factor_kernel(gram_ref, out_ref):
    out_ref[...] = gram_ref[...]
    for low in range(0, RANK, BLOCK):
        high = low + BLOCK
        panel = [out_ref[low + r : low + r + 8, :] for r in range(0, BLOCK, 8)]
        panel, unit = invert_panel(panel, low)
        out_ref[low:high, :] = jnp.concatenate(panel, axis=0)
        out_ref[low:high, low:high] = jnp.concatenate(unit, axis=0)[:, :BLOCK]
        if high < RANK:
            left = RANK - high
            a, b, c = split3(out_ref[low:high, :])
            first = jnp.concatenate([a, a, b, a, b, c], axis=0)
            second = jnp.concatenate([a, b, a, c, b, a], axis=0)
            if high % 128 == 0:
                first = first[:, high:]
            change = lax.dot_general(
                first, second, (((0,), (0,)), ((), ())), preferred_element_type=jnp.float32
            )
            change = change[change.shape[0] - left :]
            lane = lax.broadcasted_iota(jnp.int32, (left, RANK), 1)
            old = jnp.where((lane >= low) & (lane < high), 0.0, out_ref[high:, :])
            out_ref[high:, :] = old - change
    row = lax.broadcasted_iota(jnp.int32, (RANK, RANK), 0)
    lane = lax.broadcasted_iota(jnp.int32, (RANK, RANK), 1)
    out_ref[...] = jnp.where(row >= lane, out_ref[...], 0.0)


def invert_factor(gram):
    return pl.pallas_call(
        invert_factor_kernel,
        out_shape=jax.ShapeDtypeStruct((RANK, RANK), jnp.float32),
        compiler_params=pltpu.CompilerParams(vmem_limit_bytes=8 << 20),
        cost_estimate=pl.CostEstimate(flops=10_000_000_000, bytes_accessed=524288, transcendentals=0),
        name="invert_factor",
    )(gram)


def on_device(momentum, gradient, right_factor):
    core = lax.axis_index("core")
    blended = momentum + gradient.astype(jnp.float32)
    left_local = dot(blended, right_factor, ((1,), (0,)))
    left_parts = jnp.pad(left_local, ((0, 32), (0, 0))).reshape(12, 24, RANK)
    left_raw = gather(scatter_sum(left_parts, "col"), "col", 12).reshape(288, RANK)[:256]

    gram_local = dot(left_raw, left_raw, ((0,), (0,))).reshape(2, 128, RANK)
    right_local = dot(blended, left_raw, ((0,), (0,))).reshape(2, 576, RANK)
    both = jnp.concatenate([right_local, gram_local], axis=1)
    mine = lax.dynamic_index_in_dim(both, core, 0, False)
    theirs = lax.ppermute(lax.dynamic_index_in_dim(both, 1 - core, 0, False), "core", SWAP)
    part = scatter_sum((mine + theirs).reshape(4, 176, RANK), "x")
    part = scatter_sum(jnp.pad(part, ((0, 16), (0, 0))).reshape(8, 24, RANK), "y")
    part = gather(part, "y", 8).reshape(192, RANK)[:176]
    part = gather(part, "x", 4).reshape(704, RANK)

    gram_mine = part[576:]
    gram_theirs = lax.ppermute(gram_mine, "core", SWAP)
    right_mine = part[:576]
    right_theirs = lax.ppermute(right_mine, "core", SWAP)

    def in_order(own, other):
        return jnp.concatenate([jnp.where(core == 0, own, other), jnp.where(core == 0, other, own)], axis=0)

    inverse = invert_factor(in_order(gram_mine, gram_theirs))
    right_raw = in_order(right_mine, right_theirs)
    orthonormal = dot(left_raw, inverse, ((1,), (1,)))
    right_full = dot(right_raw, inverse, ((1,), (1,)))
    squares = jnp.sum(right_full * right_full, axis=0, keepdims=True)
    squares = jnp.sum(gather(squares, "col", 12), axis=(0, 1))

    new_momentum = blended - (1.0 - decay_rate) * dot(orthonormal, right_full, ((1,), (1,)))
    new_right = right_full / jnp.sqrt(squares + epsilon)
    factor = math.sqrt(ROWS * COLS / RANK)
    update = (factor * dot(orthonormal, new_right, ((1,), (1,)))).astype(jnp.bfloat16)
    return (new_momentum, new_right, update)


def solution(mesh):
    fine = Mesh(mesh.devices.reshape(4, 8, 2, 12), ("x", "y", "core", "col"))
    return jax.shard_map(
        on_device,
        mesh=fine,
        in_specs=(P(ROW, "col"), P(ROW, "col"), P("col", None)),
        out_specs=(P(ROW, "col"), P("col", None), P(ROW, "col")),
        check_vma=False,
    )
```

```python
import functools
import math

import jax
import jax.numpy as jnp
from jax import lax
from jax.experimental import pallas as pl
from jax.experimental.pallas import tpu as pltpu
from jax.sharding import Mesh
from jax.sharding import PartitionSpec as P

ROWS = 16384
COLS = 13824
RANK = 256
BLOCK = 32

decay_rate = 0.95
epsilon = 1e-06

ROW = ("x", "y", "core")
SWAP = ((0, 1), (1, 0))
HIGHEST = lax.Precision.HIGHEST


def dot(a, b, contract):
    return lax.dot_general(
        a, b, ((contract[0], contract[1]), ((), ())), precision=HIGHEST, preferred_element_type=jnp.float32
    )


def call(kernel, shapes, cost, name, limit=16, **more):
    flops, size = cost
    return pl.pallas_call(
        kernel,
        out_shape=[jax.ShapeDtypeStruct(shape, jnp.float32) for shape in shapes],
        compiler_params=pltpu.CompilerParams(vmem_limit_bytes=limit << 20),
        cost_estimate=pl.CostEstimate(flops=flops, bytes_accessed=size, transcendentals=0),
        name=name,
        **more,
    )


def exchange(parts, axes):
    return lax.all_to_all(parts, axes, 0, 0, tiled=True)


def scatter_sum(parts, axes):
    return jnp.sum(exchange(parts, axes), axis=0)


def all_sum(parts, axes, *ready):
    def kernel(in_ref, out_ref):
        total = in_ref[0]
        for i in range(1, in_ref.shape[0]):
            total = total + in_ref[i]
        for i in range(in_ref.shape[0]):
            out_ref[i] = total

    (sums,) = call(kernel, [parts.shape], (10_000_000, 2 * parts.size * 4), "add")(exchange(parts, axes))
    sums, *ready = lax.optimization_barrier((sums, *ready))
    return exchange(sums, axes), *ready


def gather(part, axes, count):
    return exchange(jnp.broadcast_to(part, (count,) + part.shape), axes)


def wide(a):
    return jnp.concatenate([a, a], axis=1)


def invert_panel(panel, low):
    pieces = len(panel)
    row8 = lax.broadcasted_iota(jnp.int32, (8, 128), 0)
    lane = lax.broadcasted_iota(jnp.int32, (8, 128), 1)
    unit = [(row8 + 8 * r == lane).astype(jnp.float32) for r in range(pieces)]
    scales = []
    for g in range(pieces):
        columns = []
        for i in range(8):
            at = low + 8 * g + i
            columns.append([
                jnp.broadcast_to(panel[r][:, at : at + 1], (8, 128)) if r >= g else None for r in range(pieces)
            ])
        pivots = jnp.zeros((8, 128), jnp.float32)
        factors = []
        for i in range(8):
            pivot = columns[i][g][i : i + 1, :]
            pivots = jnp.where(row8 == i, pivot, pivots)
            inverse = 1.0 / pivot
            factor = [columns[i][r] * inverse if r >= g else None for r in range(pieces)]
            factor[g] = jnp.where(row8 > i, factor[g], 0.0)
            factors.append(factor)
            for l in range(i + 1, 8):
                head = columns[l][g][i : i + 1, :]
                for r in range(g, pieces):
                    columns[l][r] = columns[l][r] - factor[r] * head
        for i in range(8):
            panel_row = panel[g][i : i + 1, :]
            unit_row = unit[g][i : i + 1, :]
            for r in range(g, pieces):
                panel[r] = panel[r] - wide(factors[i][r]) * panel_row
                unit[r] = unit[r] - factors[i][r] * unit_row
        scales.append(lax.rsqrt(pivots))
    panel = [panel[r] * wide(scales[r]) for r in range(pieces)]
    unit = [unit[r] * scales[r] for r in range(pieces)]
    return panel, unit


def split3(a):
    high = a.astype(jnp.bfloat16)
    rest = a - high.astype(jnp.float32)
    middle = rest.astype(jnp.bfloat16)
    return high, middle, (rest - middle.astype(jnp.float32)).astype(jnp.bfloat16)


def invert_factor_kernel(part_ref, out_ref):
    out_ref[0:64, 0:128] = part_ref[576:640, 0:128]
    out_ref[64:128, 0:128] = part_ref[576:640, 128:256]
    out_ref[0:128, 128:256] = part_ref[640:768, 0:128].T
    out_ref[128:256, :] = part_ref[640:768, :]
    for low in range(0, RANK, BLOCK):
        high = low + BLOCK
        panel = [out_ref[low + r : low + r + 8, :] for r in range(0, BLOCK, 8)]
        panel, unit = invert_panel(panel, low)
        out_ref[low:high, :] = jnp.concatenate(panel, axis=0)
        out_ref[low:high, low:high] = jnp.concatenate(unit, axis=0)[:, :BLOCK]
        if high < RANK:
            left = RANK - high
            a, b, c = split3(out_ref[low:high, :])
            first = jnp.concatenate([a, a, b, a, b, c], axis=0)
            second = jnp.concatenate([a, b, a, c, b, a], axis=0)
            if high % 128 == 0:
                first = first[:, high:]
            change = lax.dot_general(
                first, second, (((0,), (0,)), ((), ())), preferred_element_type=jnp.float32
            )
            change = change[change.shape[0] - left :]
            lane = lax.broadcasted_iota(jnp.int32, (left, RANK), 1)
            old = jnp.where((lane >= low) & (lane < high), 0.0, out_ref[high:, :])
            out_ref[high:, :] = old - change
    row = lax.broadcasted_iota(jnp.int32, (RANK, RANK), 0)
    lane = lax.broadcasted_iota(jnp.int32, (RANK, RANK), 1)
    out_ref[...] = jnp.where(row >= lane, out_ref[...], 0.0)


def split2(a):
    high = a.astype(jnp.bfloat16)
    return high, (a - high.astype(jnp.float32)).astype(jnp.bfloat16)


def dot3(a, b, contract):
    a_high, a_low = split2(a)
    b_high, b_low = split2(b)
    dims = ((contract[0], contract[1]), ((), ()))
    return (
        lax.dot_general(a_high, b_low, dims, preferred_element_type=jnp.float32)
        + lax.dot_general(a_low, b_high, dims, preferred_element_type=jnp.float32)
    ) + lax.dot_general(a_high, b_high, dims, preferred_element_type=jnp.float32)


STEP = 384


def left_kernel(product, momentum_hbm, gradient_hbm, factor_hbm, out_ref, momentum_ref, gradient_ref, factor_ref, sems):
    copies = []
    for k in range(3):
        at = pl.ds(k * STEP, STEP)
        copies.append([
            pltpu.make_async_copy(momentum_hbm.at[:, at], momentum_ref.at[k], sems.at[k, 0]),
            pltpu.make_async_copy(factor_hbm.at[at, :], factor_ref.at[k], sems.at[k, 1]),
            pltpu.make_async_copy(gradient_hbm.at[:, at], gradient_ref.at[k], sems.at[k, 2]),
        ])
        for copy in copies[k]:
            copy.start()
    out_ref[256:288, :] = jnp.zeros((32, RANK), jnp.float32)
    total = None
    for k in range(3):
        for copy in copies[k]:
            copy.wait()
        blended = momentum_ref[k] + gradient_ref[k].astype(jnp.float32)
        part = product(blended, factor_ref[k], ((1,), (0,)))
        total = part if total is None else total + part
    out_ref[0:256, :] = total


def left(momentum, gradient, right_factor, product=dot3):
    hbm = pl.BlockSpec(memory_space=pl.ANY)
    return pl.pallas_call(
        functools.partial(left_kernel, product),
        in_specs=[hbm] * 3,
        out_specs=pl.BlockSpec(memory_space=pltpu.VMEM),
        out_shape=jax.ShapeDtypeStruct((288, RANK), jnp.float32),
        scratch_shapes=[
            pltpu.VMEM((3, 256, STEP), jnp.float32),
            pltpu.VMEM((3, 256, STEP), jnp.bfloat16),
            pltpu.VMEM((3, STEP, RANK), jnp.float32),
            pltpu.SemaphoreType.DMA((3, 3)),
        ],
        compiler_params=pltpu.CompilerParams(vmem_limit_bytes=60 << 20),
        cost_estimate=pl.CostEstimate(flops=1_000_000_000, bytes_accessed=3_000_000, transcendentals=0),
        name="left",
    )(momentum, gradient, right_factor)


def fold_gram(gram):
    first = jnp.concatenate([gram[0:64, 0:128], gram[64:128, 0:128]], axis=1)
    return jnp.concatenate([first, gram[128:256, :]], axis=0)


def own_sums_kernel(blended_ref, left_ref, out_ref):
    left = left_ref[0:256, :]
    out_ref[0:576, :] = dot3(blended_ref[...], left, ((1,), (0,)))
    out_ref[576:768, :] = fold_gram(dot(left, left, ((0,), (0,))))


def other_sums_kernel(own_ref, blended_ref, left_ref, out_ref):
    left = left_ref[...]
    out_ref[0:576, :] = own_ref[0:576, :] + dot3(blended_ref[...], left, ((1,), (0,)))
    out_ref[576:768, :] = own_ref[576:768, :] + fold_gram(dot(left, left, ((0,), (0,))))


def right_kernel(core_ref, inverse_ref, left_ref, own_ref, other_ref, out_ref, squares_ref, orthonormal_ref):
    inverse = inverse_ref[...]
    own = dot3(own_ref[0:576, :], inverse, ((1,), (1,)))
    other = dot3(other_ref[...], inverse, ((1,), (1,)))
    squares = jnp.sum(own * own, axis=0, keepdims=True) + jnp.sum(other * other, axis=0, keepdims=True)
    squares_ref[...] = jnp.broadcast_to(squares.reshape(1, 1, RANK), (12, 1, RANK))

    orthonormal_ref[...] = dot3(left_ref[0:256, :], inverse, ((1,), (1,)))

    @pl.when(core_ref[0] == 0)
    def _():
        out_ref[0:576, :] = own
        out_ref[576:1152, :] = other

    @pl.when(core_ref[0] == 1)
    def _():
        out_ref[0:576, :] = other
        out_ref[576:1152, :] = own


def momentum_kernel(momentum_ref, gradient_ref, orthonormal_ref, right_ref, out_ref):
    blended = momentum_ref[...] + gradient_ref[...].astype(jnp.float32)
    product = dot3(orthonormal_ref[...], right_ref[...], ((1,), (1,)))
    out_ref[...] = blended - (1.0 - decay_rate) * product


def feedback(momentum, gradient, orthonormal, right_full):
    block = pl.BlockSpec((256, STEP), lambda i: (0, i))
    return call(
        momentum_kernel, [(256, 1152)], (1_000_000_000, 4_000_000), "momentum",
        grid=(3,),
        in_specs=[block, block, pl.BlockSpec((256, RANK), lambda i: (0, 0)), pl.BlockSpec((STEP, RANK), lambda i: (i, 0))],
        out_specs=[block],
    )(momentum, gradient, orthonormal, right_full)


def update_kernel(product, squares_ref, left_ref, right_ref, new_right_hbm, update_hbm, new_right_ref, update_ref, sems):
    squares = jnp.sum(squares_ref[...], axis=0)
    scale = jnp.sqrt(squares + epsilon)
    factor = math.sqrt(ROWS * COLS / RANK)
    copies = []
    for k in range(3):
        at = pl.ds(k * STEP, STEP)
        new_right = right_ref[at, :] / scale
        new_right_ref[at, :] = new_right
        copies.append(pltpu.make_async_copy(new_right_ref.at[at, :], new_right_hbm.at[at, :], sems.at[k, 0]))
        copies[-1].start()
        update_ref[:, at] = (factor * product(left_ref[...], new_right, ((1,), (1,)))).astype(jnp.bfloat16)
        copies.append(pltpu.make_async_copy(update_ref.at[:, at], update_hbm.at[:, at], sems.at[k, 1]))
        copies[-1].start()
    for copy in copies:
        copy.wait()


def last(squares, orthonormal, right_full, product=dot3):
    vmem = pl.BlockSpec(memory_space=pltpu.VMEM)
    return pl.pallas_call(
        functools.partial(update_kernel, product),
        in_specs=[vmem] * 3,
        out_specs=[pl.BlockSpec(memory_space=pl.ANY)] * 2,
        out_shape=[jax.ShapeDtypeStruct((1152, RANK), jnp.float32), jax.ShapeDtypeStruct((256, 1152), jnp.bfloat16)],
        scratch_shapes=[
            pltpu.VMEM((1152, RANK), jnp.float32),
            pltpu.VMEM((256, 1152), jnp.bfloat16),
            pltpu.SemaphoreType.DMA((3, 2)),
        ],
        compiler_params=pltpu.CompilerParams(vmem_limit_bytes=16 << 20),
        cost_estimate=pl.CostEstimate(flops=1_000_000_000, bytes_accessed=3_000_000, transcendentals=0),
        name="update",
    )(squares, orthonormal, right_full)


def on_device(momentum, gradient, right_factor):
    core = lax.axis_index("core")
    left_parts = left(momentum, gradient, right_factor)
    blended = momentum + gradient.astype(jnp.float32)
    kept = lax.dynamic_slice(blended, (0, core * 576), (256, 576))
    sent = lax.dynamic_slice(blended, (0, (1 - core) * 576), (256, 576))
    taken = lax.ppermute(sent, "core", SWAP)
    left_own, kept, taken = all_sum(left_parts.reshape(12, 24, RANK), "col", kept.T, taken.T)
    left_own = left_own.reshape(288, RANK)
    left_other = lax.ppermute(left_own[:256], "core", SWAP)
    cost = (500_000_000, 3_000_000)
    (own,) = call(own_sums_kernel, [(768, RANK)], cost, "own_sums")(kept, left_own)
    (sums,) = call(other_sums_kernel, [(768, RANK)], cost, "other_sums")(own, taken, left_other)
    part = scatter_sum(sums.reshape(4, 192, RANK), "x")
    (part,) = all_sum(part.reshape(8, 24, RANK), "y")
    part = part.reshape(192, RANK)
    part = gather(part, "x", 4).reshape(768, RANK)

    right_theirs = lax.ppermute(part[:576], "core", SWAP)
    (inverse,) = call(invert_factor_kernel, [(RANK, RANK)], (10_000_000_000, 524288), "inverse")(part)
    right_full, squares, orthonormal = call(
        right_kernel, [(1152, RANK), (12, 1, RANK), (256, RANK)], (1_000_000_000, 3_000_000), "right",
        in_specs=[pl.BlockSpec(memory_space=pltpu.SMEM)] + [pl.BlockSpec(memory_space=pltpu.VMEM)] * 4,
    )(core.reshape(1), inverse, left_own, part, right_theirs)
    squares = exchange(squares, "col")
    (new_momentum,) = feedback(momentum, gradient, orthonormal, right_full)
    new_right, update = last(squares, orthonormal, right_full)
    return (new_momentum, new_right, update)


def solution(mesh):
    fine = Mesh(mesh.devices.reshape(4, 8, 2, 12), ("x", "y", "core", "col"))
    return jax.shard_map(
        on_device,
        mesh=fine,
        in_specs=(P(ROW, "col"), P(ROW, "col"), P("col", None)),
        out_specs=(P(ROW, "col"), P("col", None), P(ROW, "col")),
        check_vma=False,
    )
```

```python
import functools
import math

import jax
import jax.numpy as jnp
from jax import lax
from jax.experimental import pallas as pl
from jax.experimental.pallas import tpu as pltpu
from jax.sharding import Mesh
from jax.sharding import PartitionSpec as P

ROWS = 16384
COLS = 13824
RANK = 256
BLOCK = 32

decay_rate = 0.95
epsilon = 1e-06

ROW = ("x", "y", "core")
SWAP = ((0, 1), (1, 0))
HIGHEST = lax.Precision.HIGHEST


def dot(a, b, contract):
    return lax.dot_general(
        a, b, ((contract[0], contract[1]), ((), ())), precision=HIGHEST, preferred_element_type=jnp.float32
    )


def call(kernel, shapes, cost, name, limit=16, **more):
    flops, size = cost
    return pl.pallas_call(
        kernel,
        out_shape=[jax.ShapeDtypeStruct(shape, jnp.float32) for shape in shapes],
        compiler_params=pltpu.CompilerParams(vmem_limit_bytes=limit << 20),
        cost_estimate=pl.CostEstimate(flops=flops, bytes_accessed=size, transcendentals=0),
        name=name,
        **more,
    )


def exchange(parts, axes):
    return lax.all_to_all(parts, axes, 0, 0, tiled=True)


def scatter_sum(parts, axes):
    return jnp.sum(exchange(parts, axes), axis=0)


def all_sum(parts, axes, *ready):
    def kernel(in_ref, out_ref):
        total = in_ref[0]
        for i in range(1, in_ref.shape[0]):
            total = total + in_ref[i]
        for i in range(in_ref.shape[0]):
            out_ref[i] = total

    (sums,) = call(kernel, [parts.shape], (10_000_000, 2 * parts.size * 4), "add")(exchange(parts, axes))
    sums, *ready = lax.optimization_barrier((sums, *ready))
    return exchange(sums, axes), *ready


def gather(part, axes, count):
    return exchange(jnp.broadcast_to(part, (count,) + part.shape), axes)


def wide(a):
    return jnp.concatenate([a, a], axis=1)


def invert_panel(panel, low):
    pieces = len(panel)
    row8 = lax.broadcasted_iota(jnp.int32, (8, 128), 0)
    row = lax.broadcasted_iota(jnp.int32, (8, RANK), 0)
    place = lax.broadcasted_iota(jnp.int32, (8, RANK), 1)
    scales = []

    def spread(group, start):
        return [
            [
                jnp.broadcast_to(panel[r][:, at : at + 1], (8, 128)) if r >= start else None for r in range(pieces)
            ]
            for at in range(low + 8 * group, low + 8 * group + 8)
        ]

    ahead = None
    for g in range(pieces):
        columns = ahead or spread(g, g)
        ahead = spread(g + 1, g) if g < pieces - 1 else None
        at = low + 8 * g
        inside = (place >= at) & (place < at + 8)
        for r in range(pieces):
            panel[r] = jnp.where(inside, jnp.where(place == row + at, 1.0, 0.0) if r == g else 0.0, panel[r])
        pivots = jnp.zeros((8, 128), jnp.float32)
        for i in range(8):
            pivot = columns[i][g][i : i + 1, :]
            pivots = jnp.where(row8 == i, pivot, pivots)
            inverse = 1.0 / pivot
            factor = [columns[i][r] * inverse if r >= g else None for r in range(pieces)]
            factor[g] = jnp.where(row8 > i, factor[g], 0.0)
            panel_row = jnp.broadcast_to(panel[g][i : i + 1, :], (8, RANK))
            for r in range(g, pieces):
                panel[r] = panel[r] - wide(factor[r]) * panel_row
            for column in ahead or []:
                head = column[g][i : i + 1, :]
                for r in range(g, pieces):
                    column[r] = column[r] - factor[r] * head
            for l in range(i + 1, 8):
                head = columns[l][g][i : i + 1, :]
                for r in range(g, pieces):
                    columns[l][r] = columns[l][r] - factor[r] * head
        scales.append(lax.rsqrt(pivots))
    return [panel[r] * wide(scales[r]) for r in range(pieces)]


def split3(a):
    high = a.astype(jnp.bfloat16)
    rest = a - high.astype(jnp.float32)
    middle = rest.astype(jnp.bfloat16)
    return high, middle, (rest - middle.astype(jnp.float32)).astype(jnp.bfloat16)


def invert_factor_kernel(part_ref, out_ref):
    out_ref[0:64, 0:128] = part_ref[576:640, 0:128]
    out_ref[64:128, 0:128] = part_ref[576:640, 128:256]
    out_ref[0:128, 128:256] = part_ref[640:768, 0:128].T
    out_ref[128:256, :] = part_ref[640:768, :]
    for low in range(0, RANK, BLOCK):
        high = low + BLOCK
        panel = [out_ref[low + r : low + r + 8, :] for r in range(0, BLOCK, 8)]
        panel = invert_panel(panel, low)
        out_ref[low:high, :] = jnp.concatenate(panel, axis=0)
        if high < RANK:
            left = RANK - high
            a, b, c = split3(out_ref[low:high, :])
            first = jnp.concatenate([a, a, b, a, b, c], axis=0)
            second = jnp.concatenate([a, b, a, c, b, a], axis=0)
            if high % 128 == 0:
                first = first[:, high:]
            change = lax.dot_general(
                first, second, (((0,), (0,)), ((), ())), preferred_element_type=jnp.float32
            )
            change = change[change.shape[0] - left :]
            lane = lax.broadcasted_iota(jnp.int32, (left, RANK), 1)
            old = jnp.where((lane >= low) & (lane < high), 0.0, out_ref[high:, :])
            out_ref[high:, :] = old - change
    row = lax.broadcasted_iota(jnp.int32, (RANK, RANK), 0)
    lane = lax.broadcasted_iota(jnp.int32, (RANK, RANK), 1)
    out_ref[...] = jnp.where(row >= lane, out_ref[...], 0.0)


def split2(a):
    high = a.astype(jnp.bfloat16)
    return high, (a - high.astype(jnp.float32)).astype(jnp.bfloat16)


def dot3(a, b, contract):
    a_high, a_low = split2(a)
    b_high, b_low = split2(b)
    dims = ((contract[0], contract[1]), ((), ()))
    return (
        lax.dot_general(a_high, b_low, dims, preferred_element_type=jnp.float32)
        + lax.dot_general(a_low, b_high, dims, preferred_element_type=jnp.float32)
    ) + lax.dot_general(a_high, b_high, dims, preferred_element_type=jnp.float32)


STEP = 384


def left_kernel(product, momentum_hbm, gradient_hbm, factor_hbm, out_ref, momentum_ref, gradient_ref, factor_ref, sems):
    copies = []
    for k in range(3):
        at = pl.ds(k * STEP, STEP)
        copies.append([
            pltpu.make_async_copy(momentum_hbm.at[:, at], momentum_ref.at[k], sems.at[k, 0]),
            pltpu.make_async_copy(factor_hbm.at[at, :], factor_ref.at[k], sems.at[k, 1]),
            pltpu.make_async_copy(gradient_hbm.at[:, at], gradient_ref.at[k], sems.at[k, 2]),
        ])
        for copy in copies[k]:
            copy.start()
    out_ref[256:288, :] = jnp.zeros((32, RANK), jnp.float32)
    total = None
    for k in range(3):
        for copy in copies[k]:
            copy.wait()
        blended = momentum_ref[k] + gradient_ref[k].astype(jnp.float32)
        part = product(blended, factor_ref[k], ((1,), (0,)))
        total = part if total is None else total + part
    out_ref[0:256, :] = total


def left(momentum, gradient, right_factor, product=dot3):
    hbm = pl.BlockSpec(memory_space=pl.ANY)
    return pl.pallas_call(
        functools.partial(left_kernel, product),
        in_specs=[hbm] * 3,
        out_specs=pl.BlockSpec(memory_space=pltpu.VMEM),
        out_shape=jax.ShapeDtypeStruct((288, RANK), jnp.float32),
        scratch_shapes=[
            pltpu.VMEM((3, 256, STEP), jnp.float32),
            pltpu.VMEM((3, 256, STEP), jnp.bfloat16),
            pltpu.VMEM((3, STEP, RANK), jnp.float32),
            pltpu.SemaphoreType.DMA((3, 3)),
        ],
        compiler_params=pltpu.CompilerParams(vmem_limit_bytes=60 << 20),
        cost_estimate=pl.CostEstimate(flops=1_000_000_000, bytes_accessed=3_000_000, transcendentals=0),
        name="left",
    )(momentum, gradient, right_factor)


def fold_gram(gram):
    first = jnp.concatenate([gram[0:64, 0:128], gram[64:128, 0:128]], axis=1)
    return jnp.concatenate([first, gram[128:256, :]], axis=0)


def own_sums_kernel(blended_ref, left_ref, out_ref):
    left = left_ref[0:256, :]
    out_ref[0:576, :] = dot3(blended_ref[...], left, ((1,), (0,)))
    out_ref[576:768, :] = fold_gram(dot(left, left, ((0,), (0,))))


def other_sums_kernel(own_ref, blended_ref, left_ref, out_ref):
    left = left_ref[...]
    out_ref[0:576, :] = own_ref[0:576, :] + dot3(blended_ref[...], left, ((1,), (0,)))
    out_ref[576:768, :] = own_ref[576:768, :] + fold_gram(dot(left, left, ((0,), (0,))))


def right_kernel(
    core_ref, inverse_ref, left_ref, own_ref, other_ref, out_ref, orthonormal_ref, squares_hbm, squares_ref, sem
):
    inverse = inverse_ref[...]
    own = dot3(own_ref[0:576, :], inverse, ((1,), (1,)))
    other = dot3(other_ref[...], inverse, ((1,), (1,)))
    squares = jnp.sum(own * own, axis=0, keepdims=True) + jnp.sum(other * other, axis=0, keepdims=True)
    squares_ref[...] = jnp.broadcast_to(squares.reshape(1, 1, RANK), (12, 1, RANK))
    copy = pltpu.make_async_copy(squares_ref, squares_hbm, sem)
    copy.start()
    orthonormal_ref[...] = dot3(left_ref[0:256, :], inverse, ((1,), (1,)))

    @pl.when(core_ref[0] == 0)
    def _():
        out_ref[0:576, :] = own
        out_ref[576:1152, :] = other

    @pl.when(core_ref[0] == 1)
    def _():
        out_ref[0:576, :] = other
        out_ref[576:1152, :] = own

    copy.wait()


def momentum_kernel(momentum_ref, gradient_ref, orthonormal_ref, right_ref, out_ref):
    blended = momentum_ref[...] + gradient_ref[...].astype(jnp.float32)
    product = dot3(orthonormal_ref[...], right_ref[...], ((1,), (1,)))
    out_ref[...] = blended - (1.0 - decay_rate) * product


def feedback(momentum, gradient, orthonormal, right_full):
    block = pl.BlockSpec((256, STEP), lambda i: (0, i))
    return call(
        momentum_kernel, [(256, 1152)], (1_000_000_000, 4_000_000), "momentum",
        grid=(3,),
        in_specs=[block, block, pl.BlockSpec((256, RANK), lambda i: (0, 0)), pl.BlockSpec((STEP, RANK), lambda i: (i, 0))],
        out_specs=[block],
    )(momentum, gradient, orthonormal, right_full)


def update_kernel(product, squares_ref, left_ref, right_ref, new_right_hbm, update_hbm, new_right_ref, update_ref, sems):
    squares = jnp.sum(squares_ref[...], axis=0)
    scale = jnp.sqrt(squares + epsilon)
    factor = math.sqrt(ROWS * COLS / RANK)
    copies = []
    for k in range(3):
        at = pl.ds(k * STEP, STEP)
        new_right = right_ref[at, :] / scale
        new_right_ref[at, :] = new_right
        copies.append(pltpu.make_async_copy(new_right_ref.at[at, :], new_right_hbm.at[at, :], sems.at[k, 0]))
        copies[-1].start()
        update_ref[:, at] = (factor * product(left_ref[...], new_right, ((1,), (1,)))).astype(jnp.bfloat16)
        copies.append(pltpu.make_async_copy(update_ref.at[:, at], update_hbm.at[:, at], sems.at[k, 1]))
        copies[-1].start()
    for copy in copies:
        copy.wait()


def last(squares, orthonormal, right_full, product=dot3):
    vmem = pl.BlockSpec(memory_space=pltpu.VMEM)
    return pl.pallas_call(
        functools.partial(update_kernel, product),
        in_specs=[vmem] * 3,
        out_specs=[pl.BlockSpec(memory_space=pl.ANY)] * 2,
        out_shape=[jax.ShapeDtypeStruct((1152, RANK), jnp.float32), jax.ShapeDtypeStruct((256, 1152), jnp.bfloat16)],
        scratch_shapes=[
            pltpu.VMEM((1152, RANK), jnp.float32),
            pltpu.VMEM((256, 1152), jnp.bfloat16),
            pltpu.SemaphoreType.DMA((3, 2)),
        ],
        compiler_params=pltpu.CompilerParams(vmem_limit_bytes=16 << 20),
        cost_estimate=pl.CostEstimate(flops=1_000_000_000, bytes_accessed=3_000_000, transcendentals=0),
        name="update",
    )(squares, orthonormal, right_full)


def on_device(momentum, gradient, right_factor):
    core = lax.axis_index("core")
    left_parts = left(momentum, gradient, right_factor)
    blended = momentum + gradient.astype(jnp.float32)
    kept = lax.dynamic_slice(blended, (0, core * 576), (256, 576))
    sent = lax.dynamic_slice(blended, (0, (1 - core) * 576), (256, 576))
    taken = lax.ppermute(sent, "core", SWAP)
    left_own, kept, taken = all_sum(left_parts.reshape(12, 24, RANK), "col", kept.T, taken.T)
    left_own = left_own.reshape(288, RANK)
    left_other = lax.ppermute(left_own[:256], "core", SWAP)
    cost = (500_000_000, 3_000_000)
    (own,) = call(own_sums_kernel, [(768, RANK)], cost, "own_sums")(kept, left_own)
    (sums,) = call(other_sums_kernel, [(768, RANK)], cost, "other_sums")(own, taken, left_other)
    part = scatter_sum(sums.reshape(4, 192, RANK), "x")
    (part,) = all_sum(part.reshape(8, 24, RANK), "y")
    part = part.reshape(192, RANK)
    part = gather(part, "x", 4).reshape(768, RANK)

    right_theirs = lax.ppermute(part[:576], "core", SWAP)
    (inverse,) = call(invert_factor_kernel, [(RANK, RANK)], (10_000_000_000, 524288), "inverse")(part)
    vmem = pl.BlockSpec(memory_space=pltpu.VMEM)
    right_full, orthonormal, squares = call(
        right_kernel, [(1152, RANK), (256, RANK), (12, 1, RANK)], (1_000_000_000, 3_000_000), "right",
        in_specs=[pl.BlockSpec(memory_space=pltpu.SMEM)] + [vmem] * 4,
        out_specs=[vmem, vmem, pl.BlockSpec(memory_space=pl.ANY)],
        scratch_shapes=[pltpu.VMEM((12, 1, RANK), jnp.float32), pltpu.SemaphoreType.DMA],
    )(core.reshape(1), inverse, left_own, part, right_theirs)
    squares = exchange(squares, "col")
    (new_momentum,) = feedback(momentum, gradient, orthonormal, right_full)
    new_right, update = last(squares, orthonormal, right_full)
    return (new_momentum, new_right, update)


def solution(mesh):
    fine = Mesh(mesh.devices.reshape(4, 8, 2, 12), ("x", "y", "core", "col"))
    return jax.shard_map(
        on_device,
        mesh=fine,
        in_specs=(P(ROW, "col"), P(ROW, "col"), P("col", None)),
        out_specs=(P(ROW, "col"), P("col", None), P(ROW, "col")),
        check_vma=False,
    )
```

```python
import functools
import math

import jax
import jax.numpy as jnp
from jax import lax
from jax.experimental import pallas as pl
from jax.experimental.pallas import tpu as pltpu
from jax.sharding import Mesh
from jax.sharding import PartitionSpec as P

ROWS = 16384
COLS = 13824
RANK = 256
BLOCK = 32

decay_rate = 0.95
epsilon = 1e-06

ROW = ("x", "y", "core")
COL = ("far", "near")
SWAP = ((0, 1), (1, 0))
HIGHEST = lax.Precision.HIGHEST


def dot(a, b, contract):
    return lax.dot_general(
        a, b, ((contract[0], contract[1]), ((), ())), precision=HIGHEST, preferred_element_type=jnp.float32
    )


def call(kernel, shapes, cost, name, limit=16, **more):
    flops, size = cost
    return pl.pallas_call(
        kernel,
        out_shape=[jax.ShapeDtypeStruct(shape, jnp.float32) for shape in shapes],
        compiler_params=pltpu.CompilerParams(vmem_limit_bytes=limit << 20),
        cost_estimate=pl.CostEstimate(flops=flops, bytes_accessed=size, transcendentals=0),
        name=name,
        **more,
    )


def exchange(parts, axes):
    return lax.all_to_all(parts, axes, 0, 0, tiled=True)


def scatter_sum(parts, axes):
    return jnp.sum(exchange(parts, axes), axis=0)


def add(parts, copies):
    def kernel(in_ref, out_ref):
        total = in_ref[0]
        for i in range(1, in_ref.shape[0]):
            total = total + in_ref[i]
        for i in range(copies):
            out_ref[i] = total

    shape = (copies,) + parts.shape[1:]
    return call(kernel, [shape], (10_000_000, 2 * parts.size * 4), "add")(parts)[0]


def gather(part, axes, count):
    return exchange(jnp.broadcast_to(part, (count,) + part.shape), axes)


def wide(a):
    return jnp.concatenate([a, a], axis=1)


def invert_panel(panel, low):
    pieces = len(panel)
    row8 = lax.broadcasted_iota(jnp.int32, (8, 128), 0)
    row = lax.broadcasted_iota(jnp.int32, (8, RANK), 0)
    place = lax.broadcasted_iota(jnp.int32, (8, RANK), 1)
    scales = []

    def spread(group, start):
        return [
            [
                jnp.broadcast_to(panel[r][:, at : at + 1], (8, 128)) if r >= start else None for r in range(pieces)
            ]
            for at in range(low + 8 * group, low + 8 * group + 8)
        ]

    ahead = None
    for g in range(pieces):
        columns = ahead or spread(g, g)
        ahead = spread(g + 1, g) if g < pieces - 1 else None
        at = low + 8 * g
        inside = (place >= at) & (place < at + 8)
        for r in range(pieces):
            panel[r] = jnp.where(inside, jnp.where(place == row + at, 1.0, 0.0) if r == g else 0.0, panel[r])
        pivots = jnp.zeros((8, 128), jnp.float32)
        for i in range(8):
            pivot = columns[i][g][i : i + 1, :]
            pivots = jnp.where(row8 == i, pivot, pivots)
            inverse = 1.0 / pivot
            factor = [columns[i][r] * inverse if r >= g else None for r in range(pieces)]
            factor[g] = jnp.where(row8 > i, factor[g], 0.0)
            panel_row = jnp.broadcast_to(panel[g][i : i + 1, :], (8, RANK))
            for r in range(g, pieces):
                panel[r] = panel[r] - wide(factor[r]) * panel_row
            for column in ahead or []:
                head = column[g][i : i + 1, :]
                for r in range(g, pieces):
                    column[r] = column[r] - factor[r] * head
            for l in range(i + 1, 8):
                head = columns[l][g][i : i + 1, :]
                for r in range(g, pieces):
                    columns[l][r] = columns[l][r] - factor[r] * head
        scales.append(lax.rsqrt(pivots))
    return [panel[r] * wide(scales[r]) for r in range(pieces)]


def split3(a):
    high = a.astype(jnp.bfloat16)
    rest = a - high.astype(jnp.float32)
    middle = rest.astype(jnp.bfloat16)
    return high, middle, (rest - middle.astype(jnp.float32)).astype(jnp.bfloat16)


def invert_factor_kernel(part_ref, out_ref):
    out_ref[0:64, 0:128] = part_ref[576:640, 0:128]
    out_ref[64:128, 0:128] = part_ref[576:640, 128:256]
    out_ref[0:128, 128:256] = part_ref[640:768, 0:128].T
    out_ref[128:256, :] = part_ref[640:768, :]
    for low in range(0, RANK, BLOCK):
        high = low + BLOCK
        panel = [out_ref[low + r : low + r + 8, :] for r in range(0, BLOCK, 8)]
        panel = invert_panel(panel, low)
        out_ref[low:high, :] = jnp.concatenate(panel, axis=0)
        if high < RANK:
            left = RANK - high
            a, b, c = split3(out_ref[low:high, :])
            first = jnp.concatenate([a, a, b, a, b, c], axis=0)
            second = jnp.concatenate([a, b, a, c, b, a], axis=0)
            if high % 128 == 0:
                first = first[:, high:]
            change = lax.dot_general(
                first, second, (((0,), (0,)), ((), ())), preferred_element_type=jnp.float32
            )
            change = change[change.shape[0] - left :]
            lane = lax.broadcasted_iota(jnp.int32, (left, RANK), 1)
            old = jnp.where((lane >= low) & (lane < high), 0.0, out_ref[high:, :])
            out_ref[high:, :] = old - change
    row = lax.broadcasted_iota(jnp.int32, (RANK, RANK), 0)
    lane = lax.broadcasted_iota(jnp.int32, (RANK, RANK), 1)
    out_ref[...] = jnp.where(row >= lane, out_ref[...], 0.0)


def split2(a):
    high = a.astype(jnp.bfloat16)
    return high, (a - high.astype(jnp.float32)).astype(jnp.bfloat16)


def dot3(a, b, contract):
    a_high, a_low = split2(a)
    b_high, b_low = split2(b)
    dims = ((contract[0], contract[1]), ((), ()))
    return (
        lax.dot_general(a_high, b_low, dims, preferred_element_type=jnp.float32)
        + lax.dot_general(a_low, b_high, dims, preferred_element_type=jnp.float32)
    ) + lax.dot_general(a_high, b_high, dims, preferred_element_type=jnp.float32)


STEP = 384


def left_kernel(product, momentum_hbm, gradient_hbm, factor_hbm, out_ref, momentum_ref, gradient_ref, factor_ref, sems):
    copies = []
    for k in range(3):
        at = pl.ds(k * STEP, STEP)
        copies.append([
            pltpu.make_async_copy(momentum_hbm.at[:, at], momentum_ref.at[k], sems.at[k, 0]),
            pltpu.make_async_copy(factor_hbm.at[at, :], factor_ref.at[k], sems.at[k, 1]),
            pltpu.make_async_copy(gradient_hbm.at[:, at], gradient_ref.at[k], sems.at[k, 2]),
        ])
        for copy in copies[k]:
            copy.start()
    total = None
    for k in range(3):
        for copy in copies[k]:
            copy.wait()
        blended = momentum_ref[k] + gradient_ref[k].astype(jnp.float32)
        part = product(blended, factor_ref[k], ((1,), (0,)))
        total = part if total is None else total + part
    out_ref[...] = total


def left(momentum, gradient, right_factor, product=dot3):
    hbm = pl.BlockSpec(memory_space=pl.ANY)
    return pl.pallas_call(
        functools.partial(left_kernel, product),
        in_specs=[hbm] * 3,
        out_specs=pl.BlockSpec(memory_space=pltpu.VMEM),
        out_shape=jax.ShapeDtypeStruct((256, RANK), jnp.float32),
        scratch_shapes=[
            pltpu.VMEM((3, 256, STEP), jnp.float32),
            pltpu.VMEM((3, 256, STEP), jnp.bfloat16),
            pltpu.VMEM((3, STEP, RANK), jnp.float32),
            pltpu.SemaphoreType.DMA((3, 3)),
        ],
        compiler_params=pltpu.CompilerParams(vmem_limit_bytes=60 << 20),
        cost_estimate=pl.CostEstimate(flops=1_000_000_000, bytes_accessed=3_000_000, transcendentals=0),
        name="left",
    )(momentum, gradient, right_factor)


def fold_gram(gram):
    first = jnp.concatenate([gram[0:64, 0:128], gram[64:128, 0:128]], axis=1)
    return jnp.concatenate([first, gram[128:256, :]], axis=0)


def own_sums_kernel(blended_ref, left_ref, out_ref):
    left = left_ref[...]
    out_ref[0:576, :] = dot3(blended_ref[...], left, ((1,), (0,)))
    out_ref[576:768, :] = fold_gram(dot(left, left, ((0,), (0,))))


def other_sums_kernel(own_ref, blended_ref, left_ref, out_ref):
    left = left_ref[...]
    out_ref[0:576, :] = own_ref[0:576, :] + dot3(blended_ref[...], left, ((1,), (0,)))
    out_ref[576:768, :] = own_ref[576:768, :] + fold_gram(dot(left, left, ((0,), (0,))))


def right_kernel(
    core_ref, inverse_ref, left_ref, own_ref, other_ref, out_ref, orthonormal_ref, squares_hbm, squares_ref, sem
):
    inverse = inverse_ref[...]
    own = dot3(own_ref[0:576, :], inverse, ((1,), (1,)))
    other = dot3(other_ref[...], inverse, ((1,), (1,)))
    squares = jnp.sum(own * own, axis=0, keepdims=True) + jnp.sum(other * other, axis=0, keepdims=True)
    squares_ref[...] = jnp.broadcast_to(squares.reshape(1, 1, RANK), (12, 1, RANK))
    copy = pltpu.make_async_copy(squares_ref, squares_hbm, sem)
    copy.start()
    orthonormal_ref[...] = dot3(left_ref[...], inverse, ((1,), (1,)))

    @pl.when(core_ref[0] == 0)
    def _():
        out_ref[0:576, :] = own
        out_ref[576:1152, :] = other

    @pl.when(core_ref[0] == 1)
    def _():
        out_ref[0:576, :] = other
        out_ref[576:1152, :] = own

    copy.wait()


def momentum_kernel(momentum_ref, gradient_ref, orthonormal_ref, right_ref, out_ref):
    blended = momentum_ref[...] + gradient_ref[...].astype(jnp.float32)
    product = dot3(orthonormal_ref[...], right_ref[...], ((1,), (1,)))
    out_ref[...] = blended - (1.0 - decay_rate) * product


def feedback(momentum, gradient, orthonormal, right_full):
    block = pl.BlockSpec((256, STEP), lambda i: (0, i))
    return call(
        momentum_kernel, [(256, 1152)], (1_000_000_000, 4_000_000), "momentum",
        grid=(3,),
        in_specs=[block, block, pl.BlockSpec((256, RANK), lambda i: (0, 0)), pl.BlockSpec((STEP, RANK), lambda i: (i, 0))],
        out_specs=[block],
    )(momentum, gradient, orthonormal, right_full)


def update_kernel(product, squares_ref, left_ref, right_ref, new_right_hbm, update_hbm, new_right_ref, update_ref, sems):
    squares = jnp.sum(squares_ref[...], axis=0)
    scale = jnp.sqrt(squares + epsilon)
    factor = math.sqrt(ROWS * COLS / RANK)
    copies = []
    for k in range(3):
        at = pl.ds(k * STEP, STEP)
        new_right = right_ref[at, :] / scale
        new_right_ref[at, :] = new_right
        copies.append(pltpu.make_async_copy(new_right_ref.at[at, :], new_right_hbm.at[at, :], sems.at[k, 0]))
        copies[-1].start()
        update_ref[:, at] = (factor * product(left_ref[...], new_right, ((1,), (1,)))).astype(jnp.bfloat16)
        copies.append(pltpu.make_async_copy(update_ref.at[:, at], update_hbm.at[:, at], sems.at[k, 1]))
        copies[-1].start()
    for copy in copies:
        copy.wait()


def last(squares, orthonormal, right_full, product=dot3):
    vmem = pl.BlockSpec(memory_space=pltpu.VMEM)
    return pl.pallas_call(
        functools.partial(update_kernel, product),
        in_specs=[vmem] * 3,
        out_specs=[pl.BlockSpec(memory_space=pl.ANY)] * 2,
        out_shape=[jax.ShapeDtypeStruct((1152, RANK), jnp.float32), jax.ShapeDtypeStruct((256, 1152), jnp.bfloat16)],
        scratch_shapes=[
            pltpu.VMEM((1152, RANK), jnp.float32),
            pltpu.VMEM((256, 1152), jnp.bfloat16),
            pltpu.SemaphoreType.DMA((3, 2)),
        ],
        compiler_params=pltpu.CompilerParams(vmem_limit_bytes=16 << 20),
        cost_estimate=pl.CostEstimate(flops=1_000_000_000, bytes_accessed=3_000_000, transcendentals=0),
        name="update",
    )(squares, orthonormal, right_full)


def on_device(momentum, gradient, right_factor):
    core = lax.axis_index("core")
    left_parts = left(momentum, gradient, right_factor)
    blended = momentum + gradient.astype(jnp.float32)
    sums = add(exchange(left_parts.reshape(4, 64, RANK), "near"), 3)
    sums, blended = lax.optimization_barrier((sums, blended))
    kept = lax.dynamic_slice(blended, (0, core * 576), (256, 576))
    sent = lax.dynamic_slice(blended, (0, (1 - core) * 576), (256, 576))
    taken = lax.ppermute(sent, "core", SWAP)
    sums = add(exchange(sums, "far"), 4)
    sums, kept, taken = lax.optimization_barrier((sums, kept.T, taken.T))
    left_own = exchange(sums, "near").reshape(256, RANK)
    left_other = lax.ppermute(left_own, "core", SWAP)
    cost = (500_000_000, 3_000_000)
    (own,) = call(own_sums_kernel, [(768, RANK)], cost, "own_sums")(kept, left_own)
    (sums,) = call(other_sums_kernel, [(768, RANK)], cost, "other_sums")(own, taken, left_other)
    part = scatter_sum(sums.reshape(4, 192, RANK), "x")
    part = exchange(add(exchange(part.reshape(8, 24, RANK), "y"), 8), "y").reshape(192, RANK)
    part = gather(part, "x", 4).reshape(768, RANK)

    right_theirs = lax.ppermute(part[:576], "core", SWAP)
    (inverse,) = call(invert_factor_kernel, [(RANK, RANK)], (10_000_000_000, 524288), "inverse")(part)
    vmem = pl.BlockSpec(memory_space=pltpu.VMEM)
    right_full, orthonormal, squares = call(
        right_kernel, [(1152, RANK), (256, RANK), (12, 1, RANK)], (1_000_000_000, 3_000_000), "right",
        in_specs=[pl.BlockSpec(memory_space=pltpu.SMEM)] + [vmem] * 4,
        out_specs=[vmem, vmem, pl.BlockSpec(memory_space=pl.ANY)],
        scratch_shapes=[pltpu.VMEM((12, 1, RANK), jnp.float32), pltpu.SemaphoreType.DMA],
    )(core.reshape(1), inverse, left_own, part, right_theirs)
    squares = exchange(squares, COL)
    (new_momentum,) = feedback(momentum, gradient, orthonormal, right_full)
    new_right, update = last(squares, orthonormal, right_full)
    return (new_momentum, new_right, update)


def solution(mesh):
    fine = Mesh(mesh.devices.reshape(4, 8, 2, 3, 4), ROW + COL)
    return jax.shard_map(
        on_device,
        mesh=fine,
        in_specs=(P(ROW, COL), P(ROW, COL), P(COL, None)),
        out_specs=(P(ROW, COL), P(COL, None), P(ROW, COL)),
        check_vma=False,
    )
```

```python
import functools
import math

import jax
import jax.numpy as jnp
from jax import lax
from jax.experimental import pallas as pl
from jax.experimental.pallas import tpu as pltpu
from jax.sharding import Mesh
from jax.sharding import PartitionSpec as P

ROWS = 16384
COLS = 13824
RANK = 256
BLOCK = 32

decay_rate = 0.95
epsilon = 1e-06

ROW = ("x", "y", "core")
SWAP = ((0, 1), (1, 0))
HIGHEST = lax.Precision.HIGHEST


def dot(a, b, contract):
    return lax.dot_general(
        a, b, ((contract[0], contract[1]), ((), ())), precision=HIGHEST, preferred_element_type=jnp.float32
    )


def call(kernel, shapes, cost, name, limit=16, **more):
    flops, size = cost
    return pl.pallas_call(
        kernel,
        out_shape=[jax.ShapeDtypeStruct(shape, jnp.float32) for shape in shapes],
        compiler_params=pltpu.CompilerParams(vmem_limit_bytes=limit << 20),
        cost_estimate=pl.CostEstimate(flops=flops, bytes_accessed=size, transcendentals=0),
        name=name,
        **more,
    )


def exchange(parts, axes):
    return lax.all_to_all(parts, axes, 0, 0, tiled=True)


def scatter_sum(parts, axes):
    return jnp.sum(exchange(parts, axes), axis=0)


def all_sum(parts, axes, *ready):
    def kernel(in_ref, out_ref):
        total = in_ref[0]
        for i in range(1, in_ref.shape[0]):
            total = total + in_ref[i]
        for i in range(in_ref.shape[0]):
            out_ref[i] = total

    (sums,) = call(kernel, [parts.shape], (10_000_000, 2 * parts.size * 4), "add")(exchange(parts, axes))
    sums, *ready = lax.optimization_barrier((sums, *ready))
    return exchange(sums, axes), *ready


def gather(part, axes, count):
    return exchange(jnp.broadcast_to(part, (count,) + part.shape), axes)


def wide(a):
    return jnp.concatenate([a, a], axis=1)


def invert_panel(panel, low):
    pieces = len(panel)
    row8 = lax.broadcasted_iota(jnp.int32, (8, 128), 0)
    row = lax.broadcasted_iota(jnp.int32, (8, RANK), 0)
    place = lax.broadcasted_iota(jnp.int32, (8, RANK), 1)
    scales = []

    def spread(group, start):
        return [
            [
                jnp.broadcast_to(panel[r][:, at : at + 1], (8, 128)) if r >= start else None for r in range(pieces)
            ]
            for at in range(low + 8 * group, low + 8 * group + 8)
        ]

    ahead = None
    for g in range(pieces):
        columns = ahead or spread(g, g)
        ahead = spread(g + 1, g) if g < pieces - 1 else None
        at = low + 8 * g
        inside = (place >= at) & (place < at + 8)
        for r in range(pieces):
            panel[r] = jnp.where(inside, jnp.where(place == row + at, 1.0, 0.0) if r == g else 0.0, panel[r])
        pivots = jnp.zeros((8, 128), jnp.float32)
        for i in range(8):
            pivot = columns[i][g][i : i + 1, :]
            pivots = jnp.where(row8 == i, pivot, pivots)
            inverse = 1.0 / pivot
            factor = [columns[i][r] * inverse if r >= g else None for r in range(pieces)]
            factor[g] = jnp.where(row8 > i, factor[g], 0.0)
            panel_row = jnp.broadcast_to(panel[g][i : i + 1, :], (8, RANK))
            for r in range(g, pieces):
                panel[r] = panel[r] - wide(factor[r]) * panel_row
            for column in ahead or []:
                head = column[g][i : i + 1, :]
                for r in range(g, pieces):
                    column[r] = column[r] - factor[r] * head
            for l in range(i + 1, 8):
                head = columns[l][g][i : i + 1, :]
                for r in range(g, pieces):
                    columns[l][r] = columns[l][r] - factor[r] * head
        scales.append(lax.rsqrt(pivots))
    return [panel[r] * wide(scales[r]) for r in range(pieces)]


def split3(a):
    high = a.astype(jnp.bfloat16)
    rest = a - high.astype(jnp.float32)
    middle = rest.astype(jnp.bfloat16)
    return high, middle, (rest - middle.astype(jnp.float32)).astype(jnp.bfloat16)


def invert_factor_kernel(part_ref, out_ref):
    out_ref[0:64, 0:128] = part_ref[576:640, 0:128]
    out_ref[64:128, 0:128] = part_ref[576:640, 128:256]
    out_ref[0:128, 128:256] = part_ref[640:768, 0:128].T
    out_ref[128:256, :] = part_ref[640:768, :]
    for low in range(0, RANK, BLOCK):
        high = low + BLOCK
        panel = [out_ref[low + r : low + r + 8, :] for r in range(0, BLOCK, 8)]
        panel = invert_panel(panel, low)
        out_ref[low:high, :] = jnp.concatenate(panel, axis=0)
        if high < RANK:
            left = RANK - high
            a, b, c = split3(out_ref[low:high, :])
            first = jnp.concatenate([a, a, b, a, b, c], axis=0)
            second = jnp.concatenate([a, b, a, c, b, a], axis=0)
            if high % 128 == 0:
                first = first[:, high:]
            change = lax.dot_general(
                first, second, (((0,), (0,)), ((), ())), preferred_element_type=jnp.float32
            )
            change = change[change.shape[0] - left :]
            lane = lax.broadcasted_iota(jnp.int32, (left, RANK), 1)
            old = jnp.where((lane >= low) & (lane < high), 0.0, out_ref[high:, :])
            out_ref[high:, :] = old - change
    row = lax.broadcasted_iota(jnp.int32, (RANK, RANK), 0)
    lane = lax.broadcasted_iota(jnp.int32, (RANK, RANK), 1)
    out_ref[...] = jnp.where(row >= lane, out_ref[...], 0.0)


def split2(a):
    high = a.astype(jnp.bfloat16)
    return high, (a - high.astype(jnp.float32)).astype(jnp.bfloat16)


def dot3(a, b, contract):
    a_high, a_low = split2(a)
    b_high, b_low = split2(b)
    dims = ((contract[0], contract[1]), ((), ()))
    return (
        lax.dot_general(a_high, b_low, dims, preferred_element_type=jnp.float32)
        + lax.dot_general(a_low, b_high, dims, preferred_element_type=jnp.float32)
    ) + lax.dot_general(a_high, b_high, dims, preferred_element_type=jnp.float32)


STEP = 384
PIECES = ((0, 512), (512, 384), (896, 256))


def left_kernel(product, momentum_hbm, gradient_hbm, factor_hbm, out_ref, momentum_ref, gradient_ref, factor_ref, sems):
    copies = []
    for k, (start, size) in enumerate(PIECES):
        at = pl.ds(start, size)
        copies.append([
            pltpu.make_async_copy(momentum_hbm.at[:, at], momentum_ref.at[:, at], sems.at[k, 0]),
            pltpu.make_async_copy(factor_hbm.at[at, :], factor_ref.at[at, :], sems.at[k, 1]),
            pltpu.make_async_copy(gradient_hbm.at[:, at], gradient_ref.at[:, at], sems.at[k, 2]),
        ])
        for copy in copies[k]:
            copy.start()
    out_ref[256:288, :] = jnp.zeros((32, RANK), jnp.float32)
    total = None
    for k, (start, size) in enumerate(PIECES):
        for copy in copies[k]:
            copy.wait()
        at = pl.ds(start, size)
        blended = momentum_ref[:, at] + gradient_ref[:, at].astype(jnp.float32)
        part = product(blended, factor_ref[at, :], ((1,), (0,)))
        total = part if total is None else total + part
    out_ref[0:256, :] = total


def left(momentum, gradient, right_factor, product=dot3):
    hbm = pl.BlockSpec(memory_space=pl.ANY)
    return pl.pallas_call(
        functools.partial(left_kernel, product),
        in_specs=[hbm] * 3,
        out_specs=pl.BlockSpec(memory_space=pltpu.VMEM),
        out_shape=jax.ShapeDtypeStruct((288, RANK), jnp.float32),
        scratch_shapes=[
            pltpu.VMEM((256, 1152), jnp.float32),
            pltpu.VMEM((256, 1152), jnp.bfloat16),
            pltpu.VMEM((1152, RANK), jnp.float32),
            pltpu.SemaphoreType.DMA((3, 3)),
        ],
        compiler_params=pltpu.CompilerParams(vmem_limit_bytes=60 << 20),
        cost_estimate=pl.CostEstimate(flops=1_000_000_000, bytes_accessed=3_000_000, transcendentals=0),
        name="left",
    )(momentum, gradient, right_factor)


def fold_gram(gram):
    first = jnp.concatenate([gram[0:64, 0:128], gram[64:128, 0:128]], axis=1)
    return jnp.concatenate([first, gram[128:256, :]], axis=0)


def own_sums_kernel(blended_ref, left_ref, out_ref):
    left = left_ref[0:256, :]
    out_ref[0:576, :] = dot3(blended_ref[...], left, ((1,), (0,)))
    out_ref[576:768, :] = fold_gram(dot(left, left, ((0,), (0,))))


def other_sums_kernel(own_ref, blended_ref, left_ref, out_ref):
    left = left_ref[...]
    out_ref[0:576, :] = own_ref[0:576, :] + dot3(blended_ref[...], left, ((1,), (0,)))
    out_ref[576:768, :] = own_ref[576:768, :] + fold_gram(dot(left, left, ((0,), (0,))))


def right_kernel(
    core_ref, inverse_ref, left_ref, own_ref, other_ref, out_ref, orthonormal_ref, squares_hbm, squares_ref, sem
):
    inverse = inverse_ref[...]
    own = dot3(own_ref[0:576, :], inverse, ((1,), (1,)))
    other = dot3(other_ref[...], inverse, ((1,), (1,)))
    squares = jnp.sum(own * own, axis=0, keepdims=True) + jnp.sum(other * other, axis=0, keepdims=True)
    squares_ref[...] = jnp.broadcast_to(squares.reshape(1, 1, RANK), (12, 1, RANK))
    copy = pltpu.make_async_copy(squares_ref, squares_hbm, sem)
    copy.start()
    orthonormal_ref[...] = dot3(left_ref[0:256, :], inverse, ((1,), (1,)))

    @pl.when(core_ref[0] == 0)
    def _():
        out_ref[0:576, :] = own
        out_ref[576:1152, :] = other

    @pl.when(core_ref[0] == 1)
    def _():
        out_ref[0:576, :] = other
        out_ref[576:1152, :] = own

    copy.wait()


def momentum_kernel(momentum_ref, gradient_ref, orthonormal_ref, right_ref, out_ref):
    blended = momentum_ref[...] + gradient_ref[...].astype(jnp.float32)
    product = dot3(orthonormal_ref[...], right_ref[...], ((1,), (1,)))
    out_ref[...] = blended - (1.0 - decay_rate) * product


def feedback(momentum, gradient, orthonormal, right_full):
    block = pl.BlockSpec((256, STEP), lambda i: (0, i))
    return call(
        momentum_kernel, [(256, 1152)], (1_000_000_000, 4_000_000), "momentum",
        grid=(3,),
        in_specs=[block, block, pl.BlockSpec((256, RANK), lambda i: (0, 0)), pl.BlockSpec((STEP, RANK), lambda i: (i, 0))],
        out_specs=[block],
    )(momentum, gradient, orthonormal, right_full)


def update_kernel(product, squares_ref, left_ref, right_ref, new_right_hbm, update_hbm, new_right_ref, update_ref, sems):
    squares = jnp.sum(squares_ref[...], axis=0)
    scale = jnp.sqrt(squares + epsilon)
    factor = math.sqrt(ROWS * COLS / RANK)
    copies = []
    for k in range(3):
        at = pl.ds(k * STEP, STEP)
        new_right = right_ref[at, :] / scale
        new_right_ref[at, :] = new_right
        copies.append(pltpu.make_async_copy(new_right_ref.at[at, :], new_right_hbm.at[at, :], sems.at[k, 0]))
        copies[-1].start()
        update_ref[:, at] = (factor * product(left_ref[...], new_right, ((1,), (1,)))).astype(jnp.bfloat16)
        copies.append(pltpu.make_async_copy(update_ref.at[:, at], update_hbm.at[:, at], sems.at[k, 1]))
        copies[-1].start()
    for copy in copies:
        copy.wait()


def last(squares, orthonormal, right_full, product=dot3):
    vmem = pl.BlockSpec(memory_space=pltpu.VMEM)
    return pl.pallas_call(
        functools.partial(update_kernel, product),
        in_specs=[vmem] * 3,
        out_specs=[pl.BlockSpec(memory_space=pl.ANY)] * 2,
        out_shape=[jax.ShapeDtypeStruct((1152, RANK), jnp.float32), jax.ShapeDtypeStruct((256, 1152), jnp.bfloat16)],
        scratch_shapes=[
            pltpu.VMEM((1152, RANK), jnp.float32),
            pltpu.VMEM((256, 1152), jnp.bfloat16),
            pltpu.SemaphoreType.DMA((3, 2)),
        ],
        compiler_params=pltpu.CompilerParams(vmem_limit_bytes=16 << 20),
        cost_estimate=pl.CostEstimate(flops=1_000_000_000, bytes_accessed=3_000_000, transcendentals=0),
        name="update",
    )(squares, orthonormal, right_full)


def on_device(momentum, gradient, right_factor):
    core = lax.axis_index("core")
    left_parts = left(momentum, gradient, right_factor)
    blended = momentum + gradient.astype(jnp.float32)
    kept = lax.dynamic_slice(blended, (0, core * 576), (256, 576))
    sent = lax.dynamic_slice(blended, (0, (1 - core) * 576), (256, 576))
    taken = lax.ppermute(sent, "core", SWAP)
    left_own, kept, taken = all_sum(left_parts.reshape(12, 24, RANK), "col", kept.T, taken.T)
    left_own = left_own.reshape(288, RANK)
    left_other = lax.ppermute(left_own[:256], "core", SWAP)
    cost = (500_000_000, 3_000_000)
    (own,) = call(own_sums_kernel, [(768, RANK)], cost, "own_sums")(kept, left_own)
    (sums,) = call(other_sums_kernel, [(768, RANK)], cost, "other_sums")(own, taken, left_other)
    part = scatter_sum(sums.reshape(4, 192, RANK), "x")
    (part,) = all_sum(part.reshape(8, 24, RANK), "y")
    part = part.reshape(192, RANK)
    part = gather(part, "x", 4).reshape(768, RANK)

    right_theirs = lax.ppermute(part[:576], "core", SWAP)
    (inverse,) = call(invert_factor_kernel, [(RANK, RANK)], (10_000_000_000, 524288), "inverse")(part)
    vmem = pl.BlockSpec(memory_space=pltpu.VMEM)
    right_full, orthonormal, squares = call(
        right_kernel, [(1152, RANK), (256, RANK), (12, 1, RANK)], (1_000_000_000, 3_000_000), "right",
        in_specs=[pl.BlockSpec(memory_space=pltpu.SMEM)] + [vmem] * 4,
        out_specs=[vmem, vmem, pl.BlockSpec(memory_space=pl.ANY)],
        scratch_shapes=[pltpu.VMEM((12, 1, RANK), jnp.float32), pltpu.SemaphoreType.DMA],
    )(core.reshape(1), inverse, left_own, part, right_theirs)
    squares = exchange(squares, "col")
    (new_momentum,) = feedback(momentum, gradient, orthonormal, right_full)
    new_right, update = last(squares, orthonormal, right_full)
    return (new_momentum, new_right, update)


def solution(mesh):
    fine = Mesh(mesh.devices.reshape(4, 8, 2, 12), ("x", "y", "core", "col"))
    return jax.shard_map(
        on_device,
        mesh=fine,
        in_specs=(P(ROW, "col"), P(ROW, "col"), P("col", None)),
        out_specs=(P(ROW, "col"), P("col", None), P(ROW, "col")),
        check_vma=False,
    )
```
